32 devices in a mesh: row: 4 (over y, core), col: 8 (over z, x).
Axes of the slice: x: 2, y: 2, z: 4, core: 2. Of those that a mesh axis runs over, the one named last changes fastest.
Arguments:
- block_values: bfloat16 [512, 8, 128, 128], P(('row', 'col')), as said below
- block_cols: int32 [512, 8], P(('row', 'col')), may hold values from 0 to 511, as said below
- block_present: int32 [512, 8], P(('row', 'col')), may hold values from 0 to 1, as said below
Outputs:
- sign_step: bfloat16 [512, 8, 128, 128], P('row', 'col')
The draws below stay inside these ranges and needn't reach their ends.
Inputs may be any that keep to these rules, and one draw needn't show every extreme that they name: block_cols[i, g] lies in [g * 64, (g + 1) * 64); the slot whose range holds i names i itself. The slots are paired symmetrically: if block_cols[i, g] = j then block_cols[j, i * 8 // 512] = i. `block_present`: symmetric under the pairing of block_cols; the slot of the diagonal block is always 1. `block_values`: zero where block_present is 0; the paired slot of (i, g) holds the transpose of block (i, g), so H is symmetric.
All inputs are finite; a program needn't handle non-finite values.
Results may differ from the reference program's by a relative error of at most 0.0013.
Values may be sent and summed in bfloat16 or wider, within the bound.
A program may use at most 256 MiB of HBM per device.

```python
import jax
import jax.numpy as jnp
from jax import lax

NB = 512
BS = 128
NGRP = 8
RANGES = 8


def pattern(key):
    group_width = NB // NGRP
    shifts = jax.random.randint(jax.random.fold_in(key, 11), (NGRP,), 0, group_width).astype(jnp.int32)
    density = jax.random.randint(jax.random.fold_in(key, 12), (NGRP, NGRP, 1), 3, 10)
    kept_bits = (jax.random.randint(jax.random.fold_in(key, 13), (NGRP, NGRP, group_width), 0, 10) < density).astype(jnp.int32)
    row_ids = jnp.arange(NB, dtype=jnp.int32)[:, None]
    home_group = row_ids // group_width
    position = row_ids % group_width
    slot_group = jnp.arange(NGRP, dtype=jnp.int32)[None, :]
    lower_group = jnp.minimum(home_group, slot_group)
    upper_group = jnp.maximum(home_group, slot_group)
    partner = (position + shifts[slot_group] - shifts[home_group]) % group_width
    partner = partner.astype(jnp.int32)
    lower_position = jnp.where(home_group < slot_group, position, partner)
    kept_bit = kept_bits[lower_group, upper_group, lower_position]
    present = jnp.where(home_group == slot_group, 1, kept_bit).astype(jnp.int32)
    columns = (slot_group * group_width + partner).astype(jnp.int32)
    return (columns, present)


def draw_block_cols(key, part):
    columns, present = pattern(key)
    return columns


def draw_block_present(key, part):
    columns, present = pattern(key)
    return present


def draw_block_values(key, part):
    columns, present = pattern(key)
    key = jax.random.fold_in(key, 3)
    group_width = NB // NGRP
    base_draw = jax.random.normal(key, (NB, NGRP, BS, BS), jnp.float32)
    row_ids = jnp.arange(NB, dtype=jnp.int32)[:, None]
    home_group = row_ids // group_width
    slot_group = jnp.arange(NGRP, dtype=jnp.int32)[None, :]
    mirrored = jnp.swapaxes(base_draw[columns, jnp.broadcast_to(home_group, columns.shape)], -1, -2)
    diagonal_block = (base_draw + jnp.swapaxes(base_draw, -1, -2)) * 0.70710678
    upper_side = (home_group < slot_group)[:, :, None, None]
    lower_side = (home_group > slot_group)[:, :, None, None]
    blocks = jnp.where(upper_side, base_draw, jnp.where(lower_side, mirrored, diagonal_block))
    blocks = blocks * present.astype(jnp.float32)[:, :, None, None]
    return blocks.astype(jnp.bfloat16)


def setup_inputs(seed: int = 0) -> dict:
    splits = jax.random.split(jax.random.key(seed), 4)
    block_values = draw_block_values(jax.random.fold_in(splits[3], 71), 0)
    block_cols = draw_block_cols(jax.random.fold_in(splits[3], 71), 0)
    block_present = draw_block_present(jax.random.fold_in(splits[3], 71), 0)
    return {"block_values": block_values, "block_cols": block_cols, "block_present": block_present}


def listed_product(left_blocks, right_blocks, block_cols):
    count = block_cols.shape[0] // 16

    def one_block(inputs):
        left_part, cols_part = inputs
        picked = right_blocks[cols_part]
        matches = (block_cols[cols_part] == cols_part[:, None, :]).astype(right_blocks.dtype)
        picked = picked * matches[:, :, :, None, None]
        return jnp.einsum("ihab,ihgbc->igac", left_part.astype(jnp.float32), picked.astype(jnp.float32))

    shaped = (left_blocks.reshape((count, 16) + left_blocks.shape[1:]), block_cols.reshape(count, 16, block_cols.shape[1]))
    return lax.map(one_block, shaped).reshape(left_blocks.shape)


def reference(block_values, block_cols, block_present):
    mask_half = block_present.astype(jnp.bfloat16)[:, :, None, None]
    mask_full = block_present.astype(jnp.float32)[:, :, None, None]
    weighted = block_values * mask_half
    square = (listed_product(weighted, weighted, block_cols) / 1600.0 * mask_full).astype(jnp.bfloat16)
    updated = (1.5 * weighted.astype(jnp.float32) - 0.5 * listed_product(square, weighted, block_cols)) * mask_full
    updated = updated.astype(jnp.bfloat16)
    col_width = NB // RANGES
    range_ids = jnp.arange(RANGES, dtype=jnp.int32)
    slot_of = (range_ids * NGRP) // RANGES
    taken = updated[:, slot_of]
    home_range = block_cols[:, slot_of] // col_width
    flags = (home_range == range_ids[None, :]).astype(jnp.bfloat16)
    return taken * flags[:, :, None, None]
```

```python
import functools

import jax
import jax.numpy as jnp
from jax import lax
from jax.experimental import pallas as pl
from jax.experimental.pallas import tpu as pltpu
from jax.sharding import PartitionSpec as P

MESH = pl.DeviceIdType.MESH
SLOTS = 8
SENT = 5


def sent_slot(u, index):
    tile, parity = u // 2, u % 2
    if index < 4:
        return (2 * tile + index) % SLOTS
    return u + 4 if tile < 2 else 2 * (tile - 2) + 1 - parity


def gather_kernel(sizes, own_ref, all_ref, send_sem, recv_sem, local_sem):
    nx, ny, nz = sizes
    row, col = lax.axis_index("row"), lax.axis_index("col")
    y, core = row // 2, row % 2
    z, x = col // nx, col % nx
    rows = own_ref.shape[0]
    half = rows // 2
    col_count = nx * nz

    def place(px, py, pz, pcore):
        return (py * 2 + pcore, pz * nx + px)

    def index(where):
        return where[0] * col_count + where[1]

    def x_peer(k):
        return lax.rem(x + k, nx)

    def y_peer(k):
        return lax.rem(y + k, ny)

    def z_peer(k):
        return lax.rem(z + k, nz)

    here = place(x, y, z, core)
    sibling = place(x, y, z, 1 - core)
    x_places = [place(x_peer(k), y, z, core) for k in range(1, nx)]
    y_places = [place(x, y_peer(k), z, core) for k in range(1, ny)]
    z_places = [place(x, y, z_peer(k), core) for k in range(1, nz)]
    partners = x_places + y_places + z_places + [sibling]

    barrier = pltpu.get_barrier_semaphore()
    for partner in partners:
        pl.semaphore_signal(barrier, inc=1, device_id=partner, device_id_type=MESH)
    pl.semaphore_wait(barrier, len(partners))

    sends = []

    def window(origin, part):
        return all_ref.at[pl.ds(index(origin) * rows + part * half, half)]

    def send(origin, part, target, own=False):
        source = own_ref.at[pl.ds(part * half, half)] if own else window(origin, part)
        copy = pltpu.make_async_remote_copy(
            src_ref=source,
            dst_ref=window(origin, part),
            send_sem=send_sem.at[len(sends)],
            recv_sem=recv_sem.at[index(origin) * 2 + part],
            device_id=target,
            device_id_type=MESH,
        )
        copy.start()
        sends.append(copy)

    def arrived(origin, part):
        pltpu.make_async_copy(
            window(origin, part), window(origin, part), recv_sem.at[index(origin) * 2 + part]
        ).wait()

    keep = pltpu.make_async_copy(own_ref, all_ref.at[pl.ds(index(here) * rows, rows)], local_sem)
    keep.start()

    def first(k):
        origin = place(x, y, z_peer(k), core)
        if k > 0:
            for part in range(2):
                arrived(origin, part)
        own = k == 0
        for target in x_places:
            send(origin, 0, target, own)
        for target in y_places:
            send(origin, 1, target, own)
        if own:
            for target in z_places:
                for part in range(2):
                    send(origin, part, target, own)
        for target in x_places:
            send(origin, 1, target, own)
        for target in y_places:
            send(origin, 0, target, own)
        for part in range(2):
            send(origin, part, sibling, own)

    def second(k):
        for n in range(1, nx):
            origin = place(x_peer(n), y, z_peer(k), core)
            arrived(origin, 0)
            for target in y_places:
                send(origin, 0, target)
            send(origin, 0, sibling)
        for n in range(1, ny):
            origin = place(x, y_peer(n), z_peer(k), core)
            arrived(origin, 1)
            for target in x_places:
                send(origin, 1, target)
            send(origin, 1, sibling)

    def third(k):
        for n in range(1, ny):
            origin = place(x, y_peer(n), z_peer(k), core)
            arrived(origin, 0)
            send(origin, 0, sibling)
        for n in range(1, nx):
            origin = place(x_peer(n), y, z_peer(k), core)
            arrived(origin, 1)
            send(origin, 1, sibling)
        for n in range(1, nx):
            for m in range(1, ny):
                origin = place(x_peer(n), y_peer(m), z_peer(k), core)
                for part in range(2):
                    arrived(origin, part)
                    send(origin, part, sibling)

    for k in range(nz + 2):
        if k < nz:
            first(k)
        if 0 <= k - 1 < nz:
            second(k - 1)
        if 0 <= k - 2 < nz:
            third(k - 2)

    for n in range(nx):
        for m in range(ny):
            for k in range(nz):
                origin = place(x_peer(n), y_peer(m), z_peer(k), 1 - core)
                for part in range(2):
                    arrived(origin, part)
    keep.wait()
    for copy in sends:
        copy.wait_send()


def send_count(sizes):
    nx, ny, nz = sizes
    plane = 2 * (nx - 1) + 2 * (ny - 1) + 2 * (nx - 1) * (ny - 1)
    return nz * plane + 2 * (nz - 1) + 2 * nx * ny * nz


def gather_rows(own, sizes, total):
    shape = (total,) + own.shape[1:]
    return pl.pallas_call(
        functools.partial(gather_kernel, sizes),
        out_shape=jax.ShapeDtypeStruct(shape, own.dtype),
        in_specs=[pl.BlockSpec(memory_space=pl.ANY)],
        out_specs=pl.BlockSpec(memory_space=pl.ANY),
        scratch_shapes=[
            pltpu.SemaphoreType.DMA((send_count(sizes),)),
            pltpu.SemaphoreType.DMA((2 * total // own.shape[0],)),
            pltpu.SemaphoreType.DMA,
        ],
        compiler_params=pltpu.CompilerParams(collective_id=0, has_side_effects=True),
        name="gather_rows",
    )(own)


def stored_tiles():
    tiles = []
    for t in range(4):
        u = 2 * t
        tiles.append((t, t, [[(u, 0), (u, 1)], [(u + 1, 0), (u + 1, 1)]]))
    for t in range(4):
        u = 2 * t
        tiles.append((t, (t + 1) % 4, [[(u, 2), (u, 3)], [(u + 1, 2), (u + 1, 3)]]))
    for t in range(2):
        u, v = 2 * t, 2 * t + 4
        tiles.append((t, t + 2, [[(u, 4), (v + 1, 4)], [(v, 4), (u + 1, 4)]]))
    return tiles


TILES = stored_tiles()


def sign_kernel(cols_ref, flags_ref, present_ref, home_ref, live_ref, slot_ref, *refs):
    rows = refs[:SLOTS]
    out_ref, left_ref, tile_ref, square_ref, total_ref = refs[SLOTS:]
    width = out_ref.shape[-1]
    i = pl.program_id(0)
    home = home_ref[i]
    slot = slot_ref[0]

    for a in range(SLOTS):

        @pl.when(home == a)
        def _(a=a):
            tile, parity = a // 2, a % 2
            for g in range(SLOTS):
                other, q = g // 2, g % 2
                if other == tile:
                    block = rows[a][0, q]
                elif other == (tile + 1) % 4:
                    block = rows[a][0, 2 + q]
                elif other == (tile - 1) % 4:
                    block = rows[g][0, 2 + parity].T
                else:
                    block = rows[a][0, 4] if sent_slot(a, 4) == g else rows[g][0, 4]
                    if tile >= 2:
                        block = block.T
                left_ref[g] = block

    for n, (_, _, blocks) in enumerate(TILES):
        for p in range(2):
            for q in range(2):
                u, index = blocks[p][q]
                kept = flags_ref[(i * SLOTS + u) * SENT + index] > 0
                block = rows[u][0, index]
                tile_ref[n, pl.ds(p * width, width), pl.ds(q * width, width)] = jnp.where(
                    kept, block, jnp.zeros_like(block)
                )

    def plain(left, n):
        return jnp.dot(left, tile_ref[n], preferred_element_type=jnp.float32)

    def turned(left, n):
        return lax.dot_general(
            left, tile_ref[n], (((1,), (1,)), ((), ())), preferred_element_type=jnp.float32
        )

    def column(left, t):
        total = None
        for n, (first, second, _) in enumerate(TILES):
            term = None
            if second == t:
                term = plain(left(first), n)
            elif first == t:
                term = turned(left(second), n)
            if term is not None:
                total = term if total is None else total + term
        return total

    def left_tile(t):
        return jnp.concatenate([left_ref[2 * t], left_ref[2 * t + 1]], axis=1)

    for t in range(4):
        product = column(left_tile, t) * (1.0 / 1600.0)
        for q in range(2):
            kept = present_ref[i * SLOTS + 2 * t + q] > 0
            part = product[:, q * width : (q + 1) * width]
            square_ref[2 * t + q] = jnp.where(kept, part, 0.0).astype(square_ref.dtype)

    def square_tile(t):
        return jnp.concatenate([square_ref[2 * t], square_ref[2 * t + 1]], axis=1)

    for t in range(4):

        @pl.when(slot // 2 == t)
        def _(t=t):
            product = column(square_tile, t)
            total_ref[0] = product[:, :width]
            total_ref[1] = product[:, width:]

    updated = 1.5 * left_ref[slot].astype(jnp.float32) - 0.5 * total_ref[slot % 2]
    out_ref[0, 0] = jnp.where(live_ref[i] > 0, updated, 0.0).astype(out_ref.dtype)


def sign_rows(gathered, cols, flags, present, home, live, slot):
    count = cols.shape[0]
    width = gathered.shape[-1]

    def row_spec(u):
        return pl.BlockSpec(
            (1, SENT, width, width), lambda i, cols, *rest, u=u: (cols[i * SLOTS + u], 0, 0, 0)
        )

    return pl.pallas_call(
        sign_kernel,
        grid_spec=pltpu.PrefetchScalarGridSpec(
            num_scalar_prefetch=6,
            grid=(count,),
            in_specs=[row_spec(u) for u in range(SLOTS)],
            out_specs=pl.BlockSpec((1, 1, width, width), lambda i, *rest: (i, 0, 0, 0)),
            scratch_shapes=[
                pltpu.VMEM((SLOTS, width, width), gathered.dtype),
                pltpu.VMEM((len(TILES), 2 * width, 2 * width), gathered.dtype),
                pltpu.VMEM((SLOTS, width, width), gathered.dtype),
                pltpu.VMEM((2, width, width), jnp.float32),
            ],
        ),
        out_shape=jax.ShapeDtypeStruct((count, 1, width, width), gathered.dtype),
        compiler_params=pltpu.CompilerParams(vmem_limit_bytes=40 * 2**20),
        cost_estimate=pl.CostEstimate(
            flops=count * 10 * SLOTS * 2 * SLOTS * width**3 // SLOTS,
            bytes_accessed=count * SLOTS * SENT * width * width * 2,
            transcendentals=0,
        ),
        name="sign_rows",
    )(cols.reshape(-1), flags.reshape(-1), present.reshape(-1), home, live, slot, *[gathered] * SLOTS)


def body(sizes, block_values, block_cols, block_present):
    row_count, col_count = lax.axis_size("row"), lax.axis_size("col")
    per_device = block_values.shape[0]
    panel_rows = per_device * col_count
    block_total = panel_rows * row_count
    range_width = block_total // SLOTS
    col_width = block_total // col_count
    row_here, col_here = lax.axis_index("row"), lax.axis_index("col")
    slot_here = col_here * SLOTS // col_count
    device = row_here * col_count + col_here

    codes = lax.all_gather(block_cols * 2 + block_present, ("row", "col"), axis=0, tiled=True)
    all_cols = codes // 2

    slots = jnp.array([[sent_slot(u, k) for k in range(SENT)] for u in range(SLOTS)], jnp.int32)
    range_here = device * per_device // range_width
    mine = slots[range_here]
    parts = [
        lax.dynamic_index_in_dim(block_values, mine[k], 1, keepdims=False) for k in range(SENT)
    ]
    parts[-1] = jnp.where(range_here >= SLOTS // 2, jnp.swapaxes(parts[-1], 1, 2), parts[-1])
    own = jnp.stack(parts, axis=1)
    gathered = gather_rows(own, sizes, block_total)

    first_row = row_here * panel_rows
    panel = lax.dynamic_slice_in_dim(codes, first_row, panel_rows, 0)
    cols, present = panel // 2, panel % 2
    neighbour_cols = jnp.take(all_cols, cols, axis=0)
    same = neighbour_cols == cols[:, None, :]
    flags = jnp.stack(
        [
            jnp.stack([same[:, u, sent_slot(u, k)] for k in range(SENT)], axis=1)
            for u in range(SLOTS)
        ],
        axis=1,
    ).astype(jnp.int32)
    target = lax.dynamic_index_in_dim(cols, slot_here, 1, keepdims=False)
    wanted = lax.dynamic_index_in_dim(present, slot_here, 1, keepdims=False)
    live = ((target // col_width == col_here) & (wanted > 0)).astype(jnp.int32)
    home = ((first_row + jnp.arange(panel_rows, dtype=jnp.int32)) // range_width).astype(jnp.int32)
    slot = jnp.reshape(slot_here, (1,)).astype(jnp.int32)
    return sign_rows(gathered, cols, flags, present, home, live, slot)


def solution(mesh):
    rows, cols = mesh.shape["row"], mesh.shape["col"]
    nz = 4 if cols % 4 == 0 else 1
    sizes = (cols // nz, rows // 2, nz)
    return jax.shard_map(
        functools.partial(body, sizes),
        mesh=mesh,
        in_specs=(
            P(("row", "col"), None, None, None),
            P(("row", "col"), None),
            P(("row", "col"), None),
        ),
        out_specs=P("row", "col", None, None),
        check_vma=False,
    )
```

```python
import functools

import jax
import jax.numpy as jnp
from jax import lax
from jax.experimental import pallas as pl
from jax.experimental.pallas import tpu as pltpu
from jax.sharding import PartitionSpec as P

MESH = pl.DeviceIdType.MESH
SLOTS = 8
SENT = 5


def sent_slot(u, index):
    tile, parity = u // 2, u % 2
    if index < 4:
        return (2 * tile + index) % SLOTS
    return u + 4 if tile < 2 else 2 * (tile - 2) + 1 - parity


def gather_kernel(
    sizes, own_ref, own_codes_ref, all_ref, all_codes_ref, send_sem, recv_sem, local_sem
):
    nx, ny, nz = sizes
    row, col = lax.axis_index("row"), lax.axis_index("col")
    y, core = row // 2, row % 2
    z, x = col // nx, col % nx
    rows = own_ref.shape[0]
    half = rows // 2
    col_count = nx * nz

    def place(px, py, pz, pcore):
        return (py * 2 + pcore, pz * nx + px)

    def index(where):
        return where[0] * col_count + where[1]

    def x_peer(k):
        return lax.rem(x + k, nx)

    def y_peer(k):
        return lax.rem(y + k, ny)

    upper = z // 2
    mirrored = z * (1 - upper) + (3 - z) * upper
    z_order = [z]
    if nz == 4:
        for near in (1 - mirrored, 2, 3):
            z_order.append(near * (1 - upper) + (3 - near) * upper)

    here = place(x, y, z, core)
    sibling = place(x, y, z, 1 - core)
    above = place(x, y, lax.rem(z + 1, nz), core)
    below = place(x, y, lax.rem(z + nz - 1, nz), core)
    x_places = [place(x_peer(k), y, z, core) for k in range(1, nx)]
    y_places = [place(x, y_peer(k), z, core) for k in range(1, ny)]
    partners = x_places + y_places + [sibling]
    if nz == 4:
        partners += [above, below]

    barrier = pltpu.get_barrier_semaphore()
    for partner in partners:
        pl.semaphore_signal(barrier, inc=1, device_id=partner, device_id_type=MESH)
    pl.semaphore_wait(barrier, len(partners))

    sends = []

    def windows(origin, part, own=False):
        which = index(origin)
        target = all_ref.at[pl.ds(which * rows + part * half, half)]
        source = own_ref.at[pl.ds(part * half, half)] if own else target
        refs = [(source, target, recv_sem.at[which * 3 + part])]
        if part == 0:
            codes = all_codes_ref.at[which]
            refs.append((own_codes_ref.at[0] if own else codes, codes, recv_sem.at[which * 3 + 2]))
        return refs

    def send(origin, part, target, own=False, condition=None):
        copies = []
        for source, destination, semaphore in windows(origin, part, own):
            copies.append(
                pltpu.make_async_remote_copy(
                    src_ref=source,
                    dst_ref=destination,
                    send_sem=send_sem.at[len(sends)],
                    recv_sem=semaphore,
                    device_id=target,
                    device_id_type=MESH,
                )
            )
            sends.append((copies[-1], condition))

        def start():
            for copy in copies:
                copy.start()

        if condition is None:
            start()
        else:
            pl.when(condition)(start)

    def arrived(origin, part):
        for _, target, semaphore in windows(origin, part):
            pltpu.make_async_copy(target, target, semaphore).wait()

    keep = [
        pltpu.make_async_copy(
            own_ref, all_ref.at[pl.ds(index(here) * rows, rows)], local_sem.at[0]
        ),
        pltpu.make_async_copy(own_codes_ref.at[0], all_codes_ref.at[index(here)], local_sem.at[1]),
    ]
    for copy in keep:
        copy.start()

    def first(k):
        origin = place(x, y, z_order[k], core)
        own = k == 0
        if not own:
            for part in range(2):
                arrived(origin, part)
        if nz == 4:
            going_up = z < 3 if own else (z_order[k] < z) & (z < 3)
            going_down = z > 0 if own else (z_order[k] > z) & (z > 0)
            for part in range(2):
                send(origin, part, above, own, going_up)
                send(origin, part, below, own, going_down)
        for target in x_places:
            send(origin, 0, target, own)
        for target in y_places:
            send(origin, 1, target, own)
        for target in x_places:
            send(origin, 1, target, own)
        for target in y_places:
            send(origin, 0, target, own)
        for part in range(2):
            send(origin, part, sibling, own)

    def second(k):
        for n in range(1, nx):
            origin = place(x_peer(n), y, z_order[k], core)
            arrived(origin, 0)
            for target in y_places:
                send(origin, 0, target)
            send(origin, 0, sibling)
        for n in range(1, ny):
            origin = place(x, y_peer(n), z_order[k], core)
            arrived(origin, 1)
            for target in x_places:
                send(origin, 1, target)
            send(origin, 1, sibling)

    def third(k):
        for n in range(1, ny):
            origin = place(x, y_peer(n), z_order[k], core)
            arrived(origin, 0)
            send(origin, 0, sibling)
        for n in range(1, nx):
            origin = place(x_peer(n), y, z_order[k], core)
            arrived(origin, 1)
            send(origin, 1, sibling)
        for n in range(1, nx):
            for m in range(1, ny):
                origin = place(x_peer(n), y_peer(m), z_order[k], core)
                for part in range(2):
                    arrived(origin, part)
                    send(origin, part, sibling)

    for k in range(nz + 2):
        if k < nz:
            first(k)
        if 0 <= k - 1 < nz:
            second(k - 1)
        if 0 <= k - 2 < nz:
            third(k - 2)

    for n in range(nx):
        for m in range(ny):
            for k in range(nz):
                origin = place(x_peer(n), y_peer(m), z_order[k], 1 - core)
                for part in range(2):
                    arrived(origin, part)
    for copy in keep:
        copy.wait()
    for copy, condition in sends:
        if condition is None:
            copy.wait_send()
        else:
            pl.when(condition)(copy.wait_send)


def send_count(sizes):
    nx, ny, nz = sizes
    plane = (nx - 1) + (ny - 1) + (nx - 1) * (ny - 1)
    line = 2 * nz if nz > 1 else 0
    return 3 * (nz * plane + line + nx * ny * nz)


def gather_rows(own, own_codes, sizes, total):
    devices = total // own.shape[0]
    return pl.pallas_call(
        functools.partial(gather_kernel, sizes),
        out_shape=(
            jax.ShapeDtypeStruct((total,) + own.shape[1:], own.dtype),
            jax.ShapeDtypeStruct((devices,) + own_codes.shape[1:], own_codes.dtype),
        ),
        in_specs=[pl.BlockSpec(memory_space=pl.ANY)] * 2,
        out_specs=[pl.BlockSpec(memory_space=pl.ANY)] * 2,
        scratch_shapes=[
            pltpu.SemaphoreType.DMA((send_count(sizes),)),
            pltpu.SemaphoreType.DMA((3 * devices,)),
            pltpu.SemaphoreType.DMA((2,)),
        ],
        compiler_params=pltpu.CompilerParams(collective_id=0, has_side_effects=True),
        name="gather_rows",
    )(own, own_codes)


def stored_tiles():
    tiles = []
    for t in range(4):
        u = 2 * t
        tiles.append((t, t, [[(u, 0), (u, 1)], [(u + 1, 0), (u + 1, 1)]]))
    for t in range(4):
        u = 2 * t
        tiles.append((t, (t + 1) % 4, [[(u, 2), (u, 3)], [(u + 1, 2), (u + 1, 3)]]))
    for t in range(2):
        u, v = 2 * t, 2 * t + 4
        tiles.append((t, t + 2, [[(u, 4), (v + 1, 4)], [(v, 4), (u + 1, 4)]]))
    return tiles


TILES = stored_tiles()


def sign_kernel(cols_ref, flags_ref, present_ref, home_ref, live_ref, slot_ref, *refs):
    rows = refs[:SLOTS]
    out_ref, left_ref, tile_ref, square_ref, total_ref = refs[SLOTS:]
    width = out_ref.shape[-1]
    i = pl.program_id(0)
    home = home_ref[i]
    slot = slot_ref[0]

    for a in range(SLOTS):

        @pl.when(home == a)
        def _(a=a):
            tile, parity = a // 2, a % 2
            for g in range(SLOTS):
                other, q = g // 2, g % 2
                if other == tile:
                    block = rows[a][0, q]
                elif other == (tile + 1) % 4:
                    block = rows[a][0, 2 + q]
                elif other == (tile - 1) % 4:
                    block = rows[g][0, 2 + parity].T
                else:
                    block = rows[a][0, 4] if sent_slot(a, 4) == g else rows[g][0, 4]
                    if tile >= 2:
                        block = block.T
                left_ref[g] = block

    for n, (_, _, blocks) in enumerate(TILES):
        for p in range(2):
            for q in range(2):
                u, index = blocks[p][q]
                kept = flags_ref[(i * SLOTS + u) * SENT + index] > 0
                block = rows[u][0, index]
                tile_ref[n, pl.ds(p * width, width), pl.ds(q * width, width)] = jnp.where(
                    kept, block, jnp.zeros_like(block)
                )

    def plain(left, n):
        return jnp.dot(left, tile_ref[n], preferred_element_type=jnp.float32)

    def turned(left, n):
        return lax.dot_general(
            left, tile_ref[n], (((1,), (1,)), ((), ())), preferred_element_type=jnp.float32
        )

    def column(left, t):
        total = None
        for n, (first, second, _) in enumerate(TILES):
            term = None
            if second == t:
                term = plain(left(first), n)
            elif first == t:
                term = turned(left(second), n)
            if term is not None:
                total = term if total is None else total + term
        return total

    def left_tile(t):
        return jnp.concatenate([left_ref[2 * t], left_ref[2 * t + 1]], axis=1)

    for t in range(4):
        product = column(left_tile, t) * (1.0 / 1600.0)
        for q in range(2):
            kept = present_ref[i * SLOTS + 2 * t + q] > 0
            part = product[:, q * width : (q + 1) * width]
            square_ref[2 * t + q] = jnp.where(kept, part, 0.0).astype(square_ref.dtype)

    def square_tile(t):
        return jnp.concatenate([square_ref[2 * t], square_ref[2 * t + 1]], axis=1)

    for t in range(4):

        @pl.when(slot // 2 == t)
        def _(t=t):
            product = column(square_tile, t)
            total_ref[0] = product[:, :width]
            total_ref[1] = product[:, width:]

    updated = 1.5 * left_ref[slot].astype(jnp.float32) - 0.5 * total_ref[slot % 2]
    out_ref[0, 0] = jnp.where(live_ref[i] > 0, updated, 0.0).astype(out_ref.dtype)


def sign_rows(gathered, cols, flags, present, home, live, slot):
    count = cols.shape[0]
    width = gathered.shape[-1]

    def row_spec(u):
        return pl.BlockSpec(
            (1, SENT, width, width), lambda i, cols, *rest, u=u: (cols[i * SLOTS + u], 0, 0, 0)
        )

    return pl.pallas_call(
        sign_kernel,
        grid_spec=pltpu.PrefetchScalarGridSpec(
            num_scalar_prefetch=6,
            grid=(count,),
            in_specs=[row_spec(u) for u in range(SLOTS)],
            out_specs=pl.BlockSpec((1, 1, width, width), lambda i, *rest: (i, 0, 0, 0)),
            scratch_shapes=[
                pltpu.VMEM((SLOTS, width, width), gathered.dtype),
                pltpu.VMEM((len(TILES), 2 * width, 2 * width), gathered.dtype),
                pltpu.VMEM((SLOTS, width, width), gathered.dtype),
                pltpu.VMEM((2, width, width), jnp.float32),
            ],
        ),
        out_shape=jax.ShapeDtypeStruct((count, 1, width, width), gathered.dtype),
        compiler_params=pltpu.CompilerParams(vmem_limit_bytes=40 * 2**20),
        cost_estimate=pl.CostEstimate(
            flops=count * 10 * SLOTS * 2 * SLOTS * width**3 // SLOTS,
            bytes_accessed=count * SLOTS * SENT * width * width * 2,
            transcendentals=0,
        ),
        name="sign_rows",
    )(cols.reshape(-1), flags.reshape(-1), present.reshape(-1), home, live, slot, *[gathered] * SLOTS)


def body(sizes, block_values, block_cols, block_present):
    row_count, col_count = lax.axis_size("row"), lax.axis_size("col")
    per_device = block_values.shape[0]
    panel_rows = per_device * col_count
    block_total = panel_rows * row_count
    range_width = block_total // SLOTS
    col_width = block_total // col_count
    row_here, col_here = lax.axis_index("row"), lax.axis_index("col")
    slot_here = col_here * SLOTS // col_count
    device = row_here * col_count + col_here

    slots = jnp.array([[sent_slot(u, k) for k in range(SENT)] for u in range(SLOTS)], jnp.int32)
    range_here = device * per_device // range_width
    mine = slots[range_here]
    parts = [
        lax.dynamic_index_in_dim(block_values, mine[k], 1, keepdims=False) for k in range(SENT)
    ]
    parts[-1] = jnp.where(range_here >= SLOTS // 2, jnp.swapaxes(parts[-1], 1, 2), parts[-1])
    own = jnp.stack(parts, axis=1)
    own_codes = (block_cols * 2 + block_present)[None]
    gathered, codes = gather_rows(own, own_codes, sizes, block_total)
    codes = codes.reshape(block_total, SLOTS)
    all_cols = codes // 2

    first_row = row_here * panel_rows
    panel = lax.dynamic_slice_in_dim(codes, first_row, panel_rows, 0)
    cols, present = panel // 2, panel % 2
    neighbour_cols = jnp.take(all_cols, cols, axis=0)
    same = neighbour_cols == cols[:, None, :]
    flags = jnp.stack(
        [
            jnp.stack([same[:, u, sent_slot(u, k)] for k in range(SENT)], axis=1)
            for u in range(SLOTS)
        ],
        axis=1,
    ).astype(jnp.int32)
    target = lax.dynamic_index_in_dim(cols, slot_here, 1, keepdims=False)
    wanted = lax.dynamic_index_in_dim(present, slot_here, 1, keepdims=False)
    live = ((target // col_width == col_here) & (wanted > 0)).astype(jnp.int32)
    home = ((first_row + jnp.arange(panel_rows, dtype=jnp.int32)) // range_width).astype(jnp.int32)
    slot = jnp.reshape(slot_here, (1,)).astype(jnp.int32)
    return sign_rows(gathered, cols, flags, present, home, live, slot)


def solution(mesh):
    rows, cols = mesh.shape["row"], mesh.shape["col"]
    nz = 4 if cols % 4 == 0 else 1
    sizes = (cols // nz, rows // 2, nz)
    return jax.shard_map(
        functools.partial(body, sizes),
        mesh=mesh,
        in_specs=(
            P(("row", "col"), None, None, None),
            P(("row", "col"), None),
            P(("row", "col"), None),
        ),
        out_specs=P("row", "col", None, None),
        check_vma=False,
    )
```

```python
import functools

import jax
import jax.numpy as jnp
from jax import lax
from jax.experimental import pallas as pl
from jax.experimental.pallas import tpu as pltpu
from jax.sharding import PartitionSpec as P

MESH = pl.DeviceIdType.MESH
SLOTS = 8
SENT = 5


def sent_slot(u, index):
    tile, parity = u // 2, u % 2
    if index < 4:
        return (2 * tile + index) % SLOTS
    return u + 4 if tile < 2 else 2 * (tile - 2) + 1 - parity


def gather_kernel(
    sizes, own_ref, own_codes_ref, all_ref, all_codes_ref, send_sem, recv_sem, local_sem
):
    nx, ny, nz = sizes
    row, col = lax.axis_index("row"), lax.axis_index("col")
    y, core = row // 2, row % 2
    z, x = col // nx, col % nx
    rows = own_ref.shape[0]
    last = rows // 4
    half = (rows - last) // 2
    starts, lengths = (0, half, rows - last), (half, rows - last - half, last)
    col_count = nx * nz

    def place(px, py, pz, pcore):
        return (py * 2 + pcore, pz * nx + px)

    def index(where):
        return where[0] * col_count + where[1]

    def x_peer(k):
        return lax.rem(x + k, nx)

    def y_peer(k):
        return lax.rem(y + k, ny)

    upper = z // 2
    mirrored = z * (1 - upper) + (3 - z) * upper
    z_order = [z]
    if nz == 4:
        for near in (1 - mirrored, 2, 3):
            z_order.append(near * (1 - upper) + (3 - near) * upper)

    here = place(x, y, z, core)
    sibling = place(x, y, z, 1 - core)
    above = place(x, y, lax.rem(z + 1, nz), core)
    below = place(x, y, lax.rem(z + nz - 1, nz), core)
    x_places = [place(x_peer(k), y, z, core) for k in range(1, nx)]
    y_places = [place(x, y_peer(k), z, core) for k in range(1, ny)]
    partners = x_places + y_places + [sibling]
    if nz == 4:
        partners += [above, below]

    barrier = pltpu.get_barrier_semaphore()
    for partner in partners:
        pl.semaphore_signal(barrier, inc=1, device_id=partner, device_id_type=MESH)
    pl.semaphore_wait(barrier, len(partners))

    sends = []

    def windows(origin, part, own=False):
        which = index(origin)
        target = all_ref.at[pl.ds(which * rows + starts[part], lengths[part])]
        source = own_ref.at[pl.ds(starts[part], lengths[part])] if own else target
        refs = [(source, target, recv_sem.at[which * 4 + part])]
        if part == 0:
            codes = all_codes_ref.at[which]
            refs.append((own_codes_ref.at[0] if own else codes, codes, recv_sem.at[which * 4 + 3]))
        return refs

    def send(origin, part, target, own=False, condition=None):
        copies = []
        for source, destination, semaphore in windows(origin, part, own):
            copies.append(
                pltpu.make_async_remote_copy(
                    src_ref=source,
                    dst_ref=destination,
                    send_sem=send_sem.at[len(sends)],
                    recv_sem=semaphore,
                    device_id=target,
                    device_id_type=MESH,
                )
            )
            sends.append((copies[-1], condition))

        def start():
            for copy in copies:
                copy.start()

        if condition is None:
            start()
        else:
            pl.when(condition)(start)

    def arrived(origin, part):
        for _, target, semaphore in windows(origin, part):
            pltpu.make_async_copy(target, target, semaphore).wait()

    keep = [
        pltpu.make_async_copy(
            own_ref, all_ref.at[pl.ds(index(here) * rows, rows)], local_sem.at[0]
        ),
        pltpu.make_async_copy(own_codes_ref.at[0], all_codes_ref.at[index(here)], local_sem.at[1]),
    ]
    for copy in keep:
        copy.start()

    def first(k):
        origin = place(x, y, z_order[k], core)
        own = k == 0
        if not own:
            for part in range(2):
                arrived(origin, part)
        if nz == 4:
            going_up = z < 3 if own else (z_order[k] < z) & (z < 3)
            going_down = z > 0 if own else (z_order[k] > z) & (z > 0)
            for part in range(2):
                send(origin, part, above, own, going_up)
                send(origin, part, below, own, going_down)
        for target in x_places:
            send(origin, 0, target, own)
        for target in y_places:
            send(origin, 1, target, own)
        for target in x_places:
            send(origin, 1, target, own)
        for target in y_places:
            send(origin, 0, target, own)
        for part in range(2):
            send(origin, part, sibling, own)

    def second(k):
        for n in range(1, nx):
            origin = place(x_peer(n), y, z_order[k], core)
            arrived(origin, 0)
            for target in y_places:
                send(origin, 0, target)
            send(origin, 0, sibling)
        for n in range(1, ny):
            origin = place(x, y_peer(n), z_order[k], core)
            arrived(origin, 1)
            for target in x_places:
                send(origin, 1, target)
            send(origin, 1, sibling)

    def third(k):
        for n in range(1, ny):
            origin = place(x, y_peer(n), z_order[k], core)
            arrived(origin, 0)
            send(origin, 0, sibling)
        for n in range(1, nx):
            origin = place(x_peer(n), y, z_order[k], core)
            arrived(origin, 1)
            send(origin, 1, sibling)
        for n in range(1, nx):
            for m in range(1, ny):
                origin = place(x_peer(n), y_peer(m), z_order[k], core)
                for part in range(2):
                    arrived(origin, part)
                    send(origin, part, sibling)

    def along(origin, k, own=False):
        if nz == 4:
            going_up = z < 3 if k == 0 else (z_order[k] < z) & (z < 3)
            going_down = z > 0 if k == 0 else (z_order[k] > z) & (z > 0)
            send(origin, 2, above, own, going_up)
            send(origin, 2, below, own, going_down)
        send(origin, 2, sibling, own)

    def plane_own():
        for target in x_places + y_places:
            send(here, 2, target, True)
        along(here, 0, True)

    def plane_x():
        for n in range(1, nx):
            origin = place(x_peer(n), y, z, core)
            arrived(origin, 2)
            for target in y_places:
                send(origin, 2, target)
            along(origin, 0)

    def plane_y():
        for m in range(1, ny):
            for n in range(nx):
                origin = place(x_peer(n), y_peer(m), z, core)
                arrived(origin, 2)
                along(origin, 0)

    def line(k):
        for m in range(ny):
            for n in range(nx):
                origin = place(x_peer(n), y_peer(m), z_order[k], core)
                arrived(origin, 2)
                along(origin, k)

    for k in range(nz + 2):
        if k < nz:
            first(k)
        if k == 0:
            plane_own()
        if k == 1:
            plane_x()
        if 0 <= k - 1 < nz:
            second(k - 1)
        if k == 1:
            plane_y()
        if 0 <= k - 2 < nz:
            third(k - 2)
        if 1 <= k - 2 < nz:
            line(k - 2)

    for n in range(nx):
        for m in range(ny):
            for k in range(nz):
                origin = place(x_peer(n), y_peer(m), z_order[k], 1 - core)
                for part in range(3):
                    arrived(origin, part)
    for copy in keep:
        copy.wait()
    for copy, condition in sends:
        if condition is None:
            copy.wait_send()
        else:
            pl.when(condition)(copy.wait_send)


def send_count(sizes):
    nx, ny, nz = sizes
    plane = (nx - 1) + (ny - 1) + (nx - 1) * (ny - 1)
    line = 2 * nz * (3 + nx * ny) if nz > 1 else 0
    return 3 * nz * plane + line + 4 * nx * ny * nz + plane


def gather_rows(own, own_codes, sizes, total):
    devices = total // own.shape[0]
    return pl.pallas_call(
        functools.partial(gather_kernel, sizes),
        out_shape=(
            jax.ShapeDtypeStruct((total,) + own.shape[1:], own.dtype),
            jax.ShapeDtypeStruct((devices,) + own_codes.shape[1:], own_codes.dtype),
        ),
        in_specs=[pl.BlockSpec(memory_space=pl.ANY)] * 2,
        out_specs=[pl.BlockSpec(memory_space=pl.ANY)] * 2,
        scratch_shapes=[
            pltpu.SemaphoreType.DMA((send_count(sizes),)),
            pltpu.SemaphoreType.DMA((4 * devices,)),
            pltpu.SemaphoreType.DMA((2,)),
        ],
        compiler_params=pltpu.CompilerParams(collective_id=0, has_side_effects=True),
        name="gather_rows",
    )(own, own_codes)


def stored_tiles():
    tiles = []
    for t in range(4):
        u = 2 * t
        tiles.append((t, t, [[(u, 0), (u, 1)], [(u + 1, 0), (u + 1, 1)]]))
    for t in range(4):
        u = 2 * t
        tiles.append((t, (t + 1) % 4, [[(u, 2), (u, 3)], [(u + 1, 2), (u + 1, 3)]]))
    for t in range(2):
        u, v = 2 * t, 2 * t + 4
        tiles.append((t, t + 2, [[(u, 4), (v + 1, 4)], [(v, 4), (u + 1, 4)]]))
    return tiles


TILES = stored_tiles()


def sign_kernel(cols_ref, flags_ref, present_ref, home_ref, live_ref, slot_ref, *refs):
    rows = refs[:SLOTS]
    out_ref, left_ref, tile_ref, square_ref, total_ref = refs[SLOTS:]
    width = out_ref.shape[-1]
    i = pl.program_id(0)
    home = home_ref[i]
    slot = slot_ref[0]

    for a in range(SLOTS):

        @pl.when(home == a)
        def _(a=a):
            tile, parity = a // 2, a % 2
            for g in range(SLOTS):
                other, q = g // 2, g % 2
                if other == tile:
                    block = rows[a][0, q]
                elif other == (tile + 1) % 4:
                    block = rows[a][0, 2 + q]
                elif other == (tile - 1) % 4:
                    block = rows[g][0, 2 + parity].T
                else:
                    block = rows[a][0, 4] if sent_slot(a, 4) == g else rows[g][0, 4]
                    if tile >= 2:
                        block = block.T
                left_ref[g] = block

    for n, (_, _, blocks) in enumerate(TILES):
        for p in range(2):
            for q in range(2):
                u, index = blocks[p][q]
                kept = flags_ref[(i * SLOTS + u) * SENT + index] > 0
                block = rows[u][0, index]
                tile_ref[n, pl.ds(p * width, width), pl.ds(q * width, width)] = jnp.where(
                    kept, block, jnp.zeros_like(block)
                )

    def column(left, t):
        plain = [(first, n) for n, (first, second, _) in enumerate(TILES) if second == t]
        turned = [(second, n) for n, (first, second, _) in enumerate(TILES) if first == t != second]
        total = jnp.dot(
            jnp.concatenate([left(p) for p, _ in plain], axis=1),
            jnp.concatenate([tile_ref[n] for _, n in plain], axis=0),
            preferred_element_type=jnp.float32,
        )
        return total + lax.dot_general(
            jnp.concatenate([left(p) for p, _ in turned], axis=1),
            jnp.concatenate([tile_ref[n] for _, n in turned], axis=1),
            (((1,), (1,)), ((), ())),
            preferred_element_type=jnp.float32,
        )

    def left_tile(t):
        return jnp.concatenate([left_ref[2 * t], left_ref[2 * t + 1]], axis=1)

    for t in range(4):
        product = column(left_tile, t) * (1.0 / 1600.0)
        for q in range(2):
            kept = present_ref[i * SLOTS + 2 * t + q] > 0
            part = product[:, q * width : (q + 1) * width]
            square_ref[2 * t + q] = jnp.where(kept, part, 0.0).astype(square_ref.dtype)

    def square_tile(t):
        return jnp.concatenate([square_ref[2 * t], square_ref[2 * t + 1]], axis=1)

    for t in range(4):

        @pl.when(slot // 2 == t)
        def _(t=t):
            product = column(square_tile, t)
            total_ref[0] = product[:, :width]
            total_ref[1] = product[:, width:]

    updated = 1.5 * left_ref[slot].astype(jnp.float32) - 0.5 * total_ref[slot % 2]
    out_ref[0, 0] = jnp.where(live_ref[i] > 0, updated, 0.0).astype(out_ref.dtype)


def sign_rows(gathered, cols, flags, present, home, live, slot):
    count = cols.shape[0]
    width = gathered.shape[-1]

    def row_spec(u):
        return pl.BlockSpec(
            (1, SENT, width, width), lambda i, cols, *rest, u=u: (cols[i * SLOTS + u], 0, 0, 0)
        )

    return pl.pallas_call(
        sign_kernel,
        grid_spec=pltpu.PrefetchScalarGridSpec(
            num_scalar_prefetch=6,
            grid=(count,),
            in_specs=[row_spec(u) for u in range(SLOTS)],
            out_specs=pl.BlockSpec((1, 1, width, width), lambda i, *rest: (i, 0, 0, 0)),
            scratch_shapes=[
                pltpu.VMEM((SLOTS, width, width), gathered.dtype),
                pltpu.VMEM((len(TILES), 2 * width, 2 * width), gathered.dtype),
                pltpu.VMEM((SLOTS, width, width), gathered.dtype),
                pltpu.VMEM((2, width, width), jnp.float32),
            ],
        ),
        out_shape=jax.ShapeDtypeStruct((count, 1, width, width), gathered.dtype),
        compiler_params=pltpu.CompilerParams(vmem_limit_bytes=40 * 2**20),
        cost_estimate=pl.CostEstimate(
            flops=count * 10 * SLOTS * 2 * SLOTS * width**3 // SLOTS,
            bytes_accessed=count * SLOTS * SENT * width * width * 2,
            transcendentals=0,
        ),
        name="sign_rows",
    )(cols.reshape(-1), flags.reshape(-1), present.reshape(-1), home, live, slot, *[gathered] * SLOTS)


def body(sizes, block_values, block_cols, block_present):
    row_count, col_count = lax.axis_size("row"), lax.axis_size("col")
    per_device = block_values.shape[0]
    panel_rows = per_device * col_count
    block_total = panel_rows * row_count
    range_width = block_total // SLOTS
    col_width = block_total // col_count
    row_here, col_here = lax.axis_index("row"), lax.axis_index("col")
    slot_here = col_here * SLOTS // col_count
    device = row_here * col_count + col_here

    slots = jnp.array([[sent_slot(u, k) for k in range(SENT)] for u in range(SLOTS)], jnp.int32)
    range_here = device * per_device // range_width
    mine = slots[range_here]
    parts = [
        lax.dynamic_index_in_dim(block_values, mine[k], 1, keepdims=False) for k in range(SENT)
    ]
    parts[-1] = jnp.where(range_here >= SLOTS // 2, jnp.swapaxes(parts[-1], 1, 2), parts[-1])
    own = jnp.stack(parts, axis=1)
    own_codes = (block_cols * 2 + block_present)[None]
    gathered, codes = gather_rows(own, own_codes, sizes, block_total)
    codes = codes.reshape(block_total, SLOTS)
    all_cols = codes // 2

    first_row = row_here * panel_rows
    panel = lax.dynamic_slice_in_dim(codes, first_row, panel_rows, 0)
    cols, present = panel // 2, panel % 2
    neighbour_cols = jnp.take(all_cols, cols, axis=0)
    same = neighbour_cols == cols[:, None, :]
    flags = jnp.stack(
        [
            jnp.stack([same[:, u, sent_slot(u, k)] for k in range(SENT)], axis=1)
            for u in range(SLOTS)
        ],
        axis=1,
    ).astype(jnp.int32)
    target = lax.dynamic_index_in_dim(cols, slot_here, 1, keepdims=False)
    wanted = lax.dynamic_index_in_dim(present, slot_here, 1, keepdims=False)
    live = ((target // col_width == col_here) & (wanted > 0)).astype(jnp.int32)
    home = ((first_row + jnp.arange(panel_rows, dtype=jnp.int32)) // range_width).astype(jnp.int32)
    slot = jnp.reshape(slot_here, (1,)).astype(jnp.int32)
    return sign_rows(gathered, cols, flags, present, home, live, slot)


def solution(mesh):
    rows, cols = mesh.shape["row"], mesh.shape["col"]
    nz = 4 if cols % 4 == 0 else 1
    sizes = (cols // nz, rows // 2, nz)
    return jax.shard_map(
        functools.partial(body, sizes),
        mesh=mesh,
        in_specs=(
            P(("row", "col"), None, None, None),
            P(("row", "col"), None),
            P(("row", "col"), None),
        ),
        out_specs=P("row", "col", None, None),
        check_vma=False,
    )
```
